512 devices in a mesh: dp: 32 (over x, y), tensor: 16 (over z, core).
Axes of the slice: x: 4, y: 8, z: 8, core: 2. Of those that a mesh axis runs over, the one named last changes fastest.
Arguments:
- tokens_in: bfloat16 [77824, 8192], P('dp', 'tensor'), may hold values from -6 to 6
- out_grad: bfloat16 [77824, 512], P(('dp', 'tensor')), may hold values from -0.125 to 0.125
- memory: float32 [32, 8192, 512], P('dp', 'tensor'), may hold values from -6 to 6
- right_init: float32 [512, 64], replicated, may hold values from -0.25 to 0.25
Outputs:
- left_factor: float32 [8192, 64], P('tensor')
- right_factor: float32 [512, 64], replicated
- new_memory: float32 [32, 8192, 512], P('dp', 'tensor')
The draws below stay inside these ranges and needn't reach their ends.
All inputs are finite; a program needn't handle non-finite values.
Results may differ from the reference program's by a relative error of at most 0.0003.
Values may be sent and summed in bfloat16 or wider, within the bound.
No kernel may reach another device: no remote copies, remote signals or barrier semaphores. Data moves between devices by JAX's collectives and lax.ppermute only.
A program may use at most 64 MiB of HBM per device.

```python
import math
import jax
import jax.numpy as jnp
from jax import lax

ROWS = 8192
COLS = 512
RANK = 64
ITERS = 2
TOKENS_REP = 2432
ALL_TOKENS = 77824
N_DP = 32


def steps_of(rng, dims, cuts, low, high):
    def one(position, parts):
        draws = jax.random.uniform(jax.random.fold_in(jax.random.fold_in(rng, 6), position), (parts,), jnp.float32, low / len(cuts), high / len(cuts))
        return jnp.repeat(jnp.exp(draws), dims[position] // parts).reshape((-1,) + (1,) * (len(dims) - position - 1))

    gain = one(*cuts[0])
    for cut in cuts[1:]:
        gain = gain * one(*cut)
    return gain


def scatter_about(rng, dims, width, most, split=(), kind=jnp.bfloat16):
    drawn = jax.random.normal(rng, dims, jnp.float32) * width
    if len(split) > 0:
        drawn = steps_of(rng, dims, split, -0.22, 0.18) * drawn
    return jnp.clip(drawn, min=-most, max=most).astype(kind)


def setup_inputs(seed: int = 0) -> dict:
    streams_of = jax.random.split(jax.random.key(seed), 5)
    tokens_in = scatter_about(streams_of[0], (ALL_TOKENS, ROWS), 1.0, 6.0, ((0, 32), (1, 16)))
    out_grad = scatter_about(streams_of[1], (ALL_TOKENS, COLS), TOKENS_REP ** -0.5, 0.125, ((0, 512),))
    memory = scatter_about(streams_of[2], (N_DP, ROWS, COLS), 1.0, 6.0, ((0, 32), (1, 16)), jnp.float32)
    right_init = scatter_about(streams_of[3], (COLS, RANK), COLS ** -0.5, 0.25, (), jnp.float32)
    return dict(tokens_in=tokens_in, out_grad=out_grad, memory=memory, right_init=right_init)


def right_solve(lower, matrix):
    return lax.linalg.triangular_solve(lower, matrix, left_side=False, lower=True, transpose_a=True)

def reference(tokens_in, out_grad, memory, right_init):

    def one_replica(index):
        start = index * TOKENS_REP
        rows = lax.dynamic_slice_in_dim(tokens_in, start, TOKENS_REP, 0)
        grads = lax.dynamic_slice_in_dim(out_grad, start, TOKENS_REP, 0)
        gradient = lax.dot_general(rows.astype(jnp.float32), grads.astype(jnp.float32), (((0,), (0,)), ((), ())), preferred_element_type=jnp.float32)
        return gradient + memory[index]
    merged = lax.map(one_replica, jnp.arange(N_DP, dtype=jnp.int32))
    mean_slab = lax.optimization_barrier(jnp.sum(merged, axis=0)) / N_DP
    right = right_init
    left_hat = None
    for step in range(ITERS):
        left_raw = jnp.dot(mean_slab, right, precision=lax.Precision.HIGHEST)
        gram = jnp.dot(left_raw.T, left_raw, precision=lax.Precision.HIGHEST)
        lower = jnp.linalg.cholesky(gram)
        left_hat = right_solve(lower, left_raw)
        right = jnp.dot(mean_slab.T, left_hat, precision=lax.Precision.HIGHEST)
    approx = jnp.dot(left_hat, right.T, precision=lax.Precision.HIGHEST)
    new_memory = merged - approx[None]
    return (math.sqrt(ROWS) * left_hat, right, new_memory)
```

```python
import math

import jax
import jax.numpy as jnp
from jax import lax
from jax.sharding import PartitionSpec as P

ROWS = 8192
RANK = 64
HIGH = lax.Precision.HIGHEST


def dot(a, b, ca, cb):
    return lax.dot_general(a, b, (((ca,), (cb,)), ((), ())), precision=HIGH, preferred_element_type=jnp.float32)


def exchange(pieces, axis):
    return lax.all_to_all(pieces, axis, 0, 0, tiled=False)


def fan_out(piece, axis):
    return exchange(jnp.broadcast_to(piece[None], (lax.axis_size(axis),) + piece.shape), axis)


def inverse_factor(gram):
    lower = jnp.linalg.cholesky(gram)
    eye = jnp.eye(RANK, dtype=jnp.float32)
    return lax.linalg.triangular_solve(lower, eye, left_side=True, lower=True)


def second_moment_rows(mean_slab, position):
    q, h = position // 2, position % 2
    first = h * 128 + 8 * q
    second = jnp.where(h == 1, 256, 384) + 8 * q
    step = lax.broadcasted_iota(jnp.int32, (16, 512), 0)
    wanted = jnp.where(step < 8, first + step, second + step - 8)
    pick = (lax.broadcasted_iota(jnp.int32, (16, 512), 1) == wanted).astype(jnp.float32)
    rows = dot(dot(pick, mean_slab, 1, 1), mean_slab, 1, 0)
    low = jnp.concatenate([rows[:8, :512], rows[8:, 384:]], axis=1)
    high = jnp.concatenate([rows[:8, 128:], rows[8:, 256:]], axis=1)
    return jnp.where(h == 1, high, low)


def assemble(tiles):
    tiles = tiles.reshape(16, 2, 8, 640)

    def block(h, t):
        return tiles[:, h, :, 128 * t : 128 * t + 128].reshape(128, 128)

    upper = {
        (0, 0): block(0, 0), (0, 1): block(0, 1), (0, 2): block(0, 2), (0, 3): block(0, 3),
        (1, 1): block(1, 0), (1, 2): block(1, 1), (1, 3): block(1, 2),
        (2, 2): block(1, 3), (2, 3): block(1, 4), (3, 3): block(0, 4),
    }
    return jnp.concatenate(
        [
            jnp.concatenate([upper[i, j] if i <= j else upper[j, i].T for j in range(4)], axis=1)
            for i in range(4)
        ],
        axis=0,
    )


def on_device(tokens_in, out_grad, memory, right_init):
    replicas = lax.axis_size("dp")
    merged = memory[0] + lax.dot_general(
        tokens_in,
        lax.all_gather(out_grad, "tensor", axis=0, tiled=True),
        (((0,), (0,)), ((), ())),
        preferred_element_type=jnp.float32,
    )
    mean_rows = jnp.sum(exchange(merged.reshape(replicas, -1, 512), "dp"), axis=0) / replicas
    mean_slab = fan_out(mean_rows, "dp").reshape(512, 512)
    tiles = second_moment_rows(mean_slab, lax.axis_index("dp"))
    tiles = jnp.sum(fan_out(tiles, "tensor"), axis=0)
    moment = assemble(fan_out(tiles, "dp"))

    image = dot(moment, right_init, 1, 0)
    right = dot(image, inverse_factor(dot(right_init, image, 0, 0)), 1, 1)
    image = dot(moment, right, 1, 0)
    inverse = inverse_factor(dot(right, image, 0, 0))
    left_hat = dot(dot(mean_slab, right, 1, 0), inverse, 1, 1)
    right = dot(image, inverse, 1, 1)
    new_memory = (merged - dot(left_hat, right, 1, 1))[None]
    return (math.sqrt(ROWS) * left_hat, right, new_memory)


def solution(mesh):
    return jax.shard_map(
        on_device,
        mesh=mesh,
        in_specs=(P("dp", "tensor"), P(("dp", "tensor"), None), P("dp", "tensor", None), P()),
        out_specs=(P("tensor", None), P(), P("dp", "tensor", None)),
        check_vma=False,
    )
```

```python
import math

import jax
import jax.numpy as jnp
from jax import lax
from jax.experimental import pallas as pl
from jax.experimental.pallas import tpu as pltpu
from jax.sharding import PartitionSpec as P

ROWS, COLS, RANK = 8192, 512, 64
F32 = jnp.float32
PARAMS = pltpu.CompilerParams(vmem_limit_bytes=32 * 1024 * 1024)


def dot(a, b, ca, cb):
    return lax.dot_general(
        a, b, (((ca,), (cb,)), ((), ())), precision=lax.Precision.HIGHEST, preferred_element_type=F32
    )


def shape(*dims):
    return jax.ShapeDtypeStruct(dims, F32)


def exchange(pieces, axis):
    return lax.all_to_all(pieces, axis, 0, 0, tiled=False)


def mean_kernel(parts_ref, copies_ref):
    count = parts_ref.shape[0]
    mean = jnp.sum(parts_ref[...], axis=0) * (1.0 / count)
    copies_ref[...] = jnp.broadcast_to(mean[None], copies_ref.shape)


def moment_kernel(slab_ref, copies_ref):
    position = lax.axis_index("dp")
    offset = 8 * lax.div(position, 2)
    odd = lax.rem(position, 2) == 1
    first = jnp.where(odd, 128, 0) + offset
    second = jnp.where(odd, 256, 384) + offset - 8
    step = lax.broadcasted_iota(jnp.int32, (16, COLS), 0)
    wanted = step + jnp.where(step < 8, first, second)
    pick = jnp.where(lax.broadcasted_iota(jnp.int32, (16, COLS), 1) == wanted, 1.0, 0.0)
    slab = slab_ref[...]
    rows = dot(dot(pick, slab, 1, 1), slab, 1, 0)
    low = jnp.concatenate([rows[:8, :], rows[8:, 384:]], axis=1)
    high = jnp.concatenate([rows[:8, 128:], rows[8:, 256:]], axis=1)
    tiles = jnp.where(odd, high, low)
    copies_ref[...] = jnp.broadcast_to(tiles[None], copies_ref.shape)


def sum_kernel(parts_ref, copies_ref):
    total = jnp.sum(parts_ref[...], axis=0)
    copies_ref[...] = jnp.broadcast_to(total[None], copies_ref.shape)


def inverse_factor(gram):
    lane = lax.broadcasted_iota(jnp.int32, (8, 128), 1)
    row = lax.broadcasted_iota(jnp.int32, (8, 128), 0)
    blocks = []
    for b in range(8):
        wide = jnp.concatenate([gram[8 * b : 8 * b + 8], jnp.zeros((8, RANK), F32)], axis=1)
        blocks.append(jnp.where(lane == RANK + 8 * b + row, 1.0, wide))
    for k in range(RANK):
        own, r = divmod(k, 8)
        pivot_row = jnp.broadcast_to(blocks[own][r : r + 1], (8, 128))
        scale = lax.rsqrt(jnp.broadcast_to(pivot_row[:, k : k + 1], (8, 128)))
        scaled = pivot_row * scale
        for b in range(own, 8):
            new = blocks[b] - jnp.broadcast_to(blocks[b][:, k : k + 1], (8, 128)) * scale * scaled
            if b == own:
                new = jnp.where(row > r, new, jnp.where(row == r, scaled, blocks[b]))
            blocks[b] = new
    return jnp.concatenate([block[:, RANK:] for block in blocks], axis=0)


def final_kernel(tiles_ref, slab_ref, merged_ref, right_ref, left_out, right_out, memory_out, moment):
    places = {(i, j): (i, j - i) for i in range(2) for j in range(i, 4)}
    places |= {(2, 2): (1, 3), (2, 3): (1, 4), (3, 3): (0, 4)}
    for (i, j), (h, t) in places.items():
        block = tiles_ref[:, h, :, 128 * t : 128 * t + 128].reshape(128, 128)
        moment[128 * i : 128 * i + 128, 128 * j : 128 * j + 128] = block
        if i != j:
            moment[128 * j : 128 * j + 128, 128 * i : 128 * i + 128] = block.T
    start = right_ref[...]
    image = dot(start, moment[...], 1, 0)
    right = dot(inverse_factor(dot(start, image, 1, 1)), image, 1, 0)
    image = dot(right, moment[...], 1, 0)
    left_raw = dot(right, slab_ref[...], 1, 1)
    inverse = inverse_factor(dot(right, image, 1, 1))
    left = dot(inverse, left_raw, 1, 0)
    right = dot(inverse, image, 1, 0)
    left_out[...] = math.sqrt(ROWS) * left
    right_out[...] = right
    memory_out[...] = merged_ref[...] - dot(left, right, 0, 0)


def call(kernel, out_shape, flops, moved, scratch=()):
    return pl.pallas_call(
        kernel,
        out_shape=out_shape,
        scratch_shapes=scratch,
        compiler_params=PARAMS,
        cost_estimate=pl.CostEstimate(flops=flops, bytes_accessed=moved, transcendentals=0),
    )


def on_device(tokens_in, out_grad, memory, right_init):
    replicas, pieces = lax.axis_size("dp"), lax.axis_size("tensor")
    merged = memory[0] + lax.dot_general(
        tokens_in,
        lax.all_gather(out_grad, "tensor", axis=0, tiled=True),
        (((0,), (0,)), ((), ())),
        preferred_element_type=F32,
    )
    parts = exchange(merged.reshape(replicas, -1, COLS), "dp")
    copies = call(mean_kernel, shape(32, 16, COLS), 1 << 18, 1 << 21)(parts)
    slab = exchange(copies, "dp").reshape(COLS, COLS)
    copies = call(moment_kernel, shape(pieces, 8, 640), 1 << 26, 1 << 20)(slab)
    copies = call(sum_kernel, shape(replicas, 8, 640), 1 << 17, 1 << 20)(exchange(copies, "tensor"))
    tiles = exchange(copies, "dp").reshape(16, 2, 8, 640)
    left, right, new_memory = call(
        final_kernel,
        (shape(RANK, COLS), shape(RANK, COLS), shape(COLS, COLS)),
        1 << 28,
        1 << 22,
        [pltpu.VMEM((COLS, COLS), F32)],
    )(tiles, slab, merged, right_init.T)
    return (left.T, right.T, new_memory[None])


def solution(mesh):
    return jax.shard_map(
        on_device,
        mesh=mesh,
        in_specs=(P("dp", "tensor"), P(("dp", "tensor"), None), P("dp", "tensor", None), P()),
        out_specs=(P("tensor", None), P(), P("dp", "tensor", None)),
        check_vma=False,
    )
```

```python
import functools
import math

import jax
import jax.numpy as jnp
from jax import lax
from jax.experimental import pallas as pl
from jax.experimental.pallas import tpu as pltpu
from jax.sharding import Mesh, PartitionSpec as P

ROWS, COLS, RANK, TOKENS = 8192, 512, 64, 152
F32 = jnp.float32
PARAMS = pltpu.CompilerParams(vmem_limit_bytes=32 * 1024 * 1024)


def dot(a, b, ca, cb):
    return lax.dot_general(
        a, b, (((ca,), (cb,)), ((), ())), precision=lax.Precision.HIGHEST, preferred_element_type=F32
    )


def shape(*dims):
    return jax.ShapeDtypeStruct(dims, F32)


def exchange(pieces, axis):
    return lax.all_to_all(pieces, axis, 0, 0, tiled=False)


def gradient_kernel(flip, tokens_ref, grads_ref, start_ref, out_ref):
    core = lax.axis_index("core")
    side = 1 - core if flip else core
    total = start_ref[...]
    for layer in range(tokens_ref.shape[0]):
        total += lax.dot_general(
            tokens_ref[layer, side], grads_ref[layer], (((0,), (0,)), ((), ())), preferred_element_type=F32
        )
    out_ref[...] = total


def mean_kernel(parts_ref, copies_ref):
    count = parts_ref.shape[0]
    mean = jnp.sum(parts_ref[...], axis=0) * (1.0 / count)
    copies_ref[...] = jnp.broadcast_to(mean[None], copies_ref.shape)


def moment_kernel(slab_ref, copies_ref):
    position = lax.axis_index("dp")
    offset = 8 * lax.div(position, 2)
    odd = lax.rem(position, 2) == 1
    first = jnp.where(odd, 128, 0) + offset
    second = jnp.where(odd, 256, 384) + offset - 8
    step = lax.broadcasted_iota(jnp.int32, (16, COLS), 0)
    wanted = step + jnp.where(step < 8, first, second)
    pick = jnp.where(lax.broadcasted_iota(jnp.int32, (16, COLS), 1) == wanted, 1.0, 0.0)
    slab = slab_ref[...]
    rows = dot(dot(pick, slab, 1, 1), slab, 1, 0)
    low = jnp.concatenate([rows[:8, :], rows[8:, 384:]], axis=1)
    high = jnp.concatenate([rows[:8, 128:], rows[8:, 256:]], axis=1)
    tiles = jnp.where(odd, high, low)
    copies_ref[...] = jnp.broadcast_to(tiles[None], copies_ref.shape)


def sum_kernel(parts_ref, copies_ref):
    total = jnp.sum(parts_ref[...], axis=0)
    copies_ref[...] = jnp.broadcast_to(total[None], copies_ref.shape)


def inverse_factor(gram):
    lane = lax.broadcasted_iota(jnp.int32, (8, 128), 1)
    row = lax.broadcasted_iota(jnp.int32, (8, 128), 0)
    blocks = []
    for b in range(8):
        wide = jnp.concatenate([gram[8 * b : 8 * b + 8], jnp.zeros((8, RANK), F32)], axis=1)
        blocks.append(jnp.where(lane == RANK + 8 * b + row, 1.0, wide))
    for k in range(RANK):
        own, r = divmod(k, 8)
        pivot_row = jnp.broadcast_to(blocks[own][r : r + 1], (8, 128))
        scale = lax.rsqrt(jnp.broadcast_to(pivot_row[:, k : k + 1], (8, 128)))
        scaled = pivot_row * scale
        for b in range(own, 8):
            new = blocks[b] - jnp.broadcast_to(blocks[b][:, k : k + 1], (8, 128)) * scale * scaled
            if b == own:
                new = jnp.where(row > r, new, jnp.where(row == r, scaled, blocks[b]))
            blocks[b] = new
    return jnp.concatenate([block[:, RANK:] for block in blocks], axis=0)


def final_kernel(tiles_ref, slab_ref, merged_ref, right_ref, left_out, right_out, memory_out, moment):
    places = {(i, j): (i, j - i) for i in range(2) for j in range(i, 4)}
    places |= {(2, 2): (1, 3), (2, 3): (1, 4), (3, 3): (0, 4)}
    for (i, j), (h, t) in places.items():
        block = tiles_ref[:, h, :, 128 * t : 128 * t + 128].reshape(128, 128)
        moment[128 * i : 128 * i + 128, 128 * j : 128 * j + 128] = block
        if i != j:
            moment[128 * j : 128 * j + 128, 128 * i : 128 * i + 128] = block.T
    start = right_ref[...]
    image = dot(start, moment[...], 1, 0)
    right = dot(inverse_factor(dot(start, image, 1, 1)), image, 1, 0)
    image = dot(right, moment[...], 1, 0)
    left_raw = dot(right, slab_ref[...], 1, 1)
    inverse = inverse_factor(dot(right, image, 1, 1))
    left = dot(inverse, left_raw, 1, 0)
    right = dot(inverse, image, 1, 0)
    left_out[...] = math.sqrt(ROWS) * left
    right_out[...] = right
    memory_out[...] = merged_ref[...] - dot(left, right, 0, 0)


def call(kernel, out_shape, flops, moved, scratch=()):
    return pl.pallas_call(
        kernel,
        out_shape=out_shape,
        scratch_shapes=scratch,
        compiler_params=PARAMS,
        cost_estimate=pl.CostEstimate(flops=flops, bytes_accessed=moved, transcendentals=0),
    )


def on_device(tokens_in, out_grad, memory, right_init):
    replicas, layers = lax.axis_size("dp"), lax.axis_size("z")
    pieces = 2 * layers
    tokens = tokens_in.reshape(layers, 2, TOKENS, COLS)
    own = exchange(jnp.broadcast_to(out_grad[None], (layers, TOKENS, COLS)), "z")
    other = lax.ppermute(own, "core", [(0, 1), (1, 0)])
    half = call(functools.partial(gradient_kernel, 0), shape(COLS, COLS), 1 << 29, 1 << 22)
    merged = half(tokens, own, memory[0])
    half = call(functools.partial(gradient_kernel, 1), shape(COLS, COLS), 1 << 29, 1 << 22)
    merged = half(tokens, other, merged)
    parts = exchange(merged.reshape(replicas, -1, COLS), "dp")
    copies = call(mean_kernel, shape(32, 16, COLS), 1 << 18, 1 << 21)(parts)
    slab = exchange(copies, "dp").reshape(COLS, COLS)
    copies = call(moment_kernel, shape(pieces, 8, 640), 1 << 26, 1 << 20)(slab)
    copies = call(sum_kernel, shape(replicas, 8, 640), 1 << 17, 1 << 20)(exchange(copies, ("z", "core")))
    tiles = exchange(copies, "dp").reshape(16, 2, 8, 640)
    left, right, new_memory = call(
        final_kernel,
        (shape(RANK, COLS), shape(RANK, COLS), shape(COLS, COLS)),
        1 << 28,
        1 << 22,
        [pltpu.VMEM((COLS, COLS), F32)],
    )(tiles, slab, merged, right_init.T)
    return (left.T, right.T, new_memory[None])


def solution(mesh):
    replicas, pieces = mesh.devices.shape
    split = Mesh(mesh.devices.reshape(replicas, pieces // 2, 2), ("dp", "z", "core"))
    tensor = ("z", "core")
    return jax.shard_map(
        on_device,
        mesh=split,
        in_specs=(P("dp", tensor), P(("dp", "z", "core"), None), P("dp", tensor, None), P()),
        out_specs=(P(tensor, None), P(), P("dp", tensor, None)),
        check_vma=False,
    )
```

```python
import functools
import math

import jax
import jax.numpy as jnp
from jax import lax
from jax.experimental import pallas as pl
from jax.experimental.pallas import tpu as pltpu
from jax.sharding import Mesh, PartitionSpec as P

ROWS, COLS, RANK, TOKENS = 8192, 512, 64, 152
F32 = jnp.float32
PARAMS = pltpu.CompilerParams(vmem_limit_bytes=32 * 1024 * 1024)


def dot(a, b, ca, cb):
    return lax.dot_general(
        a, b, (((ca,), (cb,)), ((), ())), precision=lax.Precision.HIGHEST, preferred_element_type=F32
    )


def shape(*dims):
    return jax.ShapeDtypeStruct(dims, F32)


def exchange(pieces, axis):
    return lax.all_to_all(pieces, axis, 0, 0, tiled=False)


def gradient_kernel(flip, tokens_ref, grads_ref, start_ref, out_ref):
    core = lax.axis_index("core")
    side = 1 - core if flip else core
    total = start_ref[...]
    for layer in range(tokens_ref.shape[0]):
        total += lax.dot_general(
            tokens_ref[layer, side], grads_ref[layer], (((0,), (0,)), ((), ())), preferred_element_type=F32
        )
    out_ref[...] = total


def mean_kernel(parts_ref, copies_ref):
    count = parts_ref.shape[0]
    mean = jnp.sum(parts_ref[...], axis=0) * (1.0 / count)
    copies_ref[...] = jnp.broadcast_to(mean[None], copies_ref.shape)


def moment_kernel(slab_ref, copies_ref):
    position = lax.axis_index("dp")
    high = lax.rem(position, 2) == 1
    first = jnp.where(high, 256, 0) + 8 * lax.div(position, 2)
    step = lax.broadcasted_iota(jnp.int32, (16, COLS), 0)
    wanted = step + jnp.where(step < 8, first, first + 120)
    pick = jnp.where(lax.broadcasted_iota(jnp.int32, (16, COLS), 1) == wanted, 1.0, 0.0)
    slab = slab_ref[...]
    rows = dot(dot(pick, slab, 1, 1), slab, 1, 0)
    for core, row in enumerate((rows[:8], rows[8:])):
        turned = jnp.concatenate([row, row], axis=1)
        near = turned[:, 128 * core : 128 * core + 384]
        far = turned[:, 128 * core + 256 : 128 * core + 640]
        tiles = jnp.where(high, far, near)
        for layer in range(copies_ref.shape[0] // 2):
            copies_ref[2 * layer + core] = tiles


def sum_kernel(parts_ref, copies_ref):
    total = jnp.sum(parts_ref[...], axis=0)
    copies_ref[...] = jnp.broadcast_to(total[None], copies_ref.shape)


def inverse_factor(gram):
    lane = lax.broadcasted_iota(jnp.int32, (8, 128), 1)
    row = lax.broadcasted_iota(jnp.int32, (8, 128), 0)
    blocks = []
    for b in range(8):
        wide = jnp.concatenate([gram[8 * b : 8 * b + 8], jnp.zeros((8, RANK), F32)], axis=1)
        blocks.append(jnp.where(lane == RANK + 8 * b + row, 1.0, wide))

    def spread(part):
        return jnp.broadcast_to(part, (8, 128))

    for p in range(8):
        rows = [spread(blocks[p][i : i + 1]) for i in range(8)]
        entry = {(i, j): spread(rows[i][:, 8 * p + j : 8 * p + j + 1]) for i in range(8) for j in range(i, 8)}
        columns = {
            b: [spread(blocks[b][:, 8 * p + j : 8 * p + j + 1]) for j in range(8)] for b in range(p + 1, 8)
        }
        for i in range(8):
            scale = lax.rsqrt(entry[i, i])
            rows[i] = rows[i] * scale
            for column in columns.values():
                column[i] = column[i] * scale
            factor = {j: entry[i, j] * scale for j in range(i + 1, 8)}
            for k in range(i + 1, 8):
                for j in range(k, 8):
                    entry[k, j] = entry[k, j] - factor[k] * factor[j]
                rows[k] = rows[k] - factor[k] * rows[i]
                for column in columns.values():
                    column[k] = column[k] - factor[k] * column[i]
        for b, column in columns.items():
            for i in range(8):
                blocks[b] = blocks[b] - column[i] * rows[i]
        done = rows[0]
        for i in range(1, 8):
            done = jnp.where(row == i, rows[i], done)
        blocks[p] = done
    return jnp.concatenate([block[:, RANK:] for block in blocks], axis=0)


def final_kernel(tiles_ref, slab_ref, merged_ref, right_ref, left_out, right_out, memory_out, moment):
    for b in range(4):
        for j in range(3):
            block = tiles_ref[b % 2, :, b // 2, :, 128 * j : 128 * j + 128].reshape(128, 128)
            to = (b + j) % 4
            moment[128 * b : 128 * b + 128, 128 * to : 128 * to + 128] = block
            if j == 1:
                moment[128 * to : 128 * to + 128, 128 * b : 128 * b + 128] = block.T
    start = right_ref[...]
    image = dot(start, moment[...], 1, 0)
    right = dot(inverse_factor(dot(start, image, 1, 1)), image, 1, 0)
    image = dot(right, moment[...], 1, 0)
    left_raw = dot(right, slab_ref[...], 1, 1)
    inverse = inverse_factor(dot(right, image, 1, 1))
    left = dot(inverse, left_raw, 1, 0)
    right = dot(inverse, image, 1, 0)
    left_out[...] = math.sqrt(ROWS) * left
    right_out[...] = right
    memory_out[...] = merged_ref[...] - dot(left, right, 0, 0)


def call(kernel, out_shape, flops, moved, scratch=()):
    return pl.pallas_call(
        kernel,
        out_shape=out_shape,
        scratch_shapes=scratch,
        compiler_params=PARAMS,
        cost_estimate=pl.CostEstimate(flops=flops, bytes_accessed=moved, transcendentals=0),
    )


def on_device(tokens_in, out_grad, memory, right_init):
    replicas, layers = lax.axis_size("dp"), lax.axis_size("z")
    pieces = 2 * layers
    tokens = tokens_in.reshape(layers, 2, TOKENS, COLS)
    own = exchange(jnp.broadcast_to(out_grad[None], (layers, TOKENS, COLS)), "z")
    other = lax.ppermute(own, "core", [(0, 1), (1, 0)])
    half = call(functools.partial(gradient_kernel, 0), shape(COLS, COLS), 1 << 29, 1 << 22)
    merged = half(tokens, own, memory[0])
    half = call(functools.partial(gradient_kernel, 1), shape(COLS, COLS), 1 << 29, 1 << 22)
    merged = half(tokens, other, merged)
    parts = exchange(merged.reshape(replicas, -1, COLS), "dp")
    copies = call(mean_kernel, shape(32, 16, COLS), 1 << 18, 1 << 21)(parts)
    slab = exchange(copies, "dp").reshape(COLS, COLS)
    copies = call(moment_kernel, shape(pieces, 8, 384), 1 << 26, 1 << 20)(slab)
    copies = call(sum_kernel, shape(replicas, 8, 384), 1 << 17, 1 << 20)(exchange(copies, ("z", "core")))
    tiles = lax.all_gather(exchange(copies, "dp"), "core").reshape(2, 16, 2, 8, 384)
    left, right, new_memory = call(
        final_kernel,
        (shape(RANK, COLS), shape(RANK, COLS), shape(COLS, COLS)),
        1 << 28,
        1 << 22,
        [pltpu.VMEM((COLS, COLS), F32)],
    )(tiles, slab, merged, right_init.T)
    return (left.T, right.T, new_memory[None])


def solution(mesh):
    replicas, pieces = mesh.devices.shape
    split = Mesh(mesh.devices.reshape(replicas, pieces // 2, 2), ("dp", "z", "core"))
    tensor = ("z", "core")
    return jax.shard_map(
        on_device,
        mesh=split,
        in_specs=(P("dp", tensor), P(("dp", "z", "core"), None), P("dp", tensor, None), P()),
        out_specs=(P(tensor, None), P(), P("dp", tensor, None)),
        check_vma=False,
    )
```

```python
import functools
import math

import jax
import jax.numpy as jnp
from jax import lax
from jax.experimental import pallas as pl
from jax.experimental.pallas import tpu as pltpu
from jax.sharding import Mesh, PartitionSpec as P

ROWS, COLS, RANK, TOKENS = 8192, 512, 64, 152
F32 = jnp.float32
SPLIT = 384
PARAMS = pltpu.CompilerParams(vmem_limit_bytes=32 * 1024 * 1024)


def dot(a, b, ca, cb):
    return lax.dot_general(
        a, b, (((ca,), (cb,)), ((), ())), precision=lax.Precision.HIGHEST, preferred_element_type=F32
    )


def shape(*dims):
    return jax.ShapeDtypeStruct(dims, F32)


def exchange(pieces, axis):
    return lax.all_to_all(pieces, axis, 0, 0, tiled=False)


def product_kernel(tokens_ref, grads_ref, start_ref, out_ref):
    out_ref[...] = start_ref[...] + lax.dot_general(
        tokens_ref[...], grads_ref[...], (((0,), (0,)), ((), ())), preferred_element_type=F32
    )


def gradient_kernel(flip, tokens_ref, grads_ref, start_ref, *refs):
    *tail_refs, out_ref = refs
    core = lax.axis_index("core")
    side = 1 - core if flip else core
    total = start_ref[...]
    for layer in range(tokens_ref.shape[0]):
        total += lax.dot_general(
            tokens_ref[layer, side], grads_ref[layer], (((0,), (0,)), ((), ())), preferred_element_type=F32
        )
    out_ref[:, :SPLIT] = total
    for tail_ref in tail_refs:
        out_ref[:, SPLIT:] = tail_ref[...]


def mean_kernel(parts_ref, copies_ref):
    count = parts_ref.shape[0]
    mean = jnp.sum(parts_ref[...], axis=0) * (1.0 / count)
    copies_ref[...] = jnp.broadcast_to(mean[None], copies_ref.shape)


def moment_kernel(slab_ref, copies_ref):
    position = lax.axis_index("dp")
    high = lax.rem(position, 2) == 1
    first = jnp.where(high, 256, 0) + 8 * lax.div(position, 2)
    step = lax.broadcasted_iota(jnp.int32, (16, COLS), 0)
    wanted = step + jnp.where(step < 8, first, first + 120)
    pick = jnp.where(lax.broadcasted_iota(jnp.int32, (16, COLS), 1) == wanted, 1.0, 0.0)
    slab = slab_ref[...]
    rows = dot(dot(pick, slab, 1, 1), slab, 1, 0)
    for core, row in enumerate((rows[:8], rows[8:])):
        turned = jnp.concatenate([row, row], axis=1)
        near = turned[:, 128 * core : 128 * core + 384]
        far = turned[:, 128 * core + 256 : 128 * core + 640]
        tiles = jnp.where(high, far, near)
        for layer in range(copies_ref.shape[0] // 2):
            copies_ref[2 * layer + core] = tiles


def sum_kernel(parts_ref, copies_ref):
    total = jnp.sum(parts_ref[...], axis=0)
    copies_ref[...] = jnp.broadcast_to(total[None], copies_ref.shape)


def inverse_factor(gram):
    lane = lax.broadcasted_iota(jnp.int32, (8, 128), 1)
    row = lax.broadcasted_iota(jnp.int32, (8, 128), 0)
    blocks = []
    for b in range(8):
        wide = jnp.concatenate([gram[8 * b : 8 * b + 8], jnp.zeros((8, RANK), F32)], axis=1)
        blocks.append(jnp.where(lane == RANK + 8 * b + row, 1.0, wide))

    def spread(part):
        return jnp.broadcast_to(part, (8, 128))

    for p in range(8):
        rows = [spread(blocks[p][i : i + 1]) for i in range(8)]
        entry = {(i, j): spread(rows[i][:, 8 * p + j : 8 * p + j + 1]) for i in range(8) for j in range(i, 8)}
        columns = {
            b: [spread(blocks[b][:, 8 * p + j : 8 * p + j + 1]) for j in range(8)] for b in range(p + 1, 8)
        }
        for i in range(8):
            scale = lax.rsqrt(entry[i, i])
            rows[i] = rows[i] * scale
            for column in columns.values():
                column[i] = column[i] * scale
            factor = {j: entry[i, j] * scale for j in range(i + 1, 8)}
            for k in range(i + 1, 8):
                for j in range(k, 8):
                    entry[k, j] = entry[k, j] - factor[k] * factor[j]
                rows[k] = rows[k] - factor[k] * rows[i]
                for column in columns.values():
                    column[k] = column[k] - factor[k] * column[i]
        for b, column in columns.items():
            for i in range(8):
                blocks[b] = blocks[b] - column[i] * rows[i]
        done = rows[0]
        for i in range(1, 8):
            done = jnp.where(row == i, rows[i], done)
        blocks[p] = done
    return jnp.concatenate([block[:, RANK:] for block in blocks], axis=0)


def final_kernel(tiles_ref, slab_ref, merged_ref, right_ref, left_out, right_out, memory_out, moment):
    for b in range(4):
        for j in range(3):
            block = tiles_ref[b % 2, :, b // 2, :, 128 * j : 128 * j + 128].reshape(128, 128)
            to = (b + j) % 4
            moment[128 * b : 128 * b + 128, 128 * to : 128 * to + 128] = block
            if j == 1:
                moment[128 * to : 128 * to + 128, 128 * b : 128 * b + 128] = block.T
    start = right_ref[...]
    image = dot(start, moment[...], 1, 0)
    right = dot(inverse_factor(dot(start, image, 1, 1)), image, 1, 0)
    image = dot(right, moment[...], 1, 0)
    left_raw = dot(right, slab_ref[...], 1, 1)
    inverse = inverse_factor(dot(right, image, 1, 1))
    left = dot(inverse, left_raw, 1, 0)
    right = dot(inverse, image, 1, 0)
    left_out[...] = math.sqrt(ROWS) * left
    right_out[...] = right
    memory_out[...] = merged_ref[...] - dot(left, right, 0, 0)


def call(kernel, out_shape, flops, moved, scratch=()):
    return pl.pallas_call(
        kernel,
        out_shape=out_shape,
        scratch_shapes=scratch,
        compiler_params=PARAMS,
        cost_estimate=pl.CostEstimate(flops=flops, bytes_accessed=moved, transcendentals=0),
    )


def on_device(tokens_in, out_grad, memory, right_init):
    replicas, layers = lax.axis_size("dp"), lax.axis_size("z")
    pieces = 2 * layers
    tokens = tokens_in.reshape(layers, 2, TOKENS, COLS)
    own = exchange(jnp.broadcast_to(out_grad[None, :, :SPLIT], (layers, TOKENS, SPLIT)), "z")
    grads = lax.all_gather(out_grad[:, SPLIT:], ("z", "core"), axis=0, tiled=True)
    tail = call(product_kernel, shape(COLS, COLS - SPLIT), 1 << 28, 1 << 22)(tokens_in, grads, memory[0, :, SPLIT:])
    own, tail = lax.optimization_barrier((own, tail))
    other = lax.ppermute(own, "core", [(0, 1), (1, 0)])
    half = call(functools.partial(gradient_kernel, 0), shape(COLS, SPLIT), 1 << 29, 1 << 22)
    merged = half(tokens, own, memory[0, :, :SPLIT])
    whole = call(functools.partial(gradient_kernel, 1), shape(COLS, COLS), 1 << 29, 1 << 22)
    merged = whole(tokens, other, merged, tail)
    parts = exchange(merged.reshape(replicas, -1, COLS), "dp")
    copies = call(mean_kernel, shape(32, 16, COLS), 1 << 18, 1 << 21)(parts)
    slab = exchange(copies, "dp").reshape(COLS, COLS)
    copies = call(moment_kernel, shape(pieces, 8, 384), 1 << 26, 1 << 20)(slab)
    copies = call(sum_kernel, shape(replicas, 8, 384), 1 << 17, 1 << 20)(exchange(copies, ("z", "core")))
    tiles = lax.all_gather(exchange(copies, "dp"), "core").reshape(2, 16, 2, 8, 384)
    left, right, new_memory = call(
        final_kernel,
        (shape(RANK, COLS), shape(RANK, COLS), shape(COLS, COLS)),
        1 << 28,
        1 << 22,
        [pltpu.VMEM((COLS, COLS), F32)],
    )(tiles, slab, merged, right_init.T)
    return (left.T, right.T, new_memory[None])


def solution(mesh):
    replicas, pieces = mesh.devices.shape
    split = Mesh(mesh.devices.reshape(replicas, pieces // 2, 2), ("dp", "z", "core"))
    tensor = ("z", "core")
    return jax.shard_map(
        on_device,
        mesh=split,
        in_specs=(P("dp", tensor), P(("dp", "z", "core"), None), P("dp", tensor, None), P()),
        out_specs=(P(tensor, None), P(), P("dp", tensor, None)),
        check_vma=False,
    )
```

```python
import functools
import math

import jax
import jax.numpy as jnp
from jax import lax
from jax.experimental import pallas as pl
from jax.experimental.pallas import tpu as pltpu
from jax.sharding import Mesh, PartitionSpec as P

ROWS, COLS, RANK, TOKENS = 8192, 512, 64, 152
F32 = jnp.float32
PARAMS = pltpu.CompilerParams(vmem_limit_bytes=32 * 1024 * 1024)


def dot(a, b, ca, cb):
    return lax.dot_general(
        a, b, (((ca,), (cb,)), ((), ())), precision=lax.Precision.HIGHEST, preferred_element_type=F32
    )


def shape(*dims):
    return jax.ShapeDtypeStruct(dims, F32)


def exchange(pieces, axis):
    return lax.all_to_all(pieces, axis, 0, 0, tiled=False)


def gradient_kernel(flip, tokens_ref, grads_ref, start_ref, out_ref):
    core = lax.axis_index("core")
    side = 1 - core if flip else core
    total = start_ref[...]
    for layer in range(tokens_ref.shape[0]):
        total += lax.dot_general(
            tokens_ref[layer, side], grads_ref[layer], (((0,), (0,)), ((), ())), preferred_element_type=F32
        )
    out_ref[...] = total


def partial_kernel(parts_ref, part_ref):
    part_ref[...] = jnp.sum(parts_ref[...], axis=0)


def mean_kernel(count, parts_ref, copies_ref):
    mean = jnp.sum(parts_ref[...], axis=0) * (1.0 / count)
    copies_ref[...] = jnp.broadcast_to(mean[None], copies_ref.shape)


def moment_kernel(slab_ref, copies_ref):
    position = lax.axis_index("x") * lax.axis_size("y") + lax.axis_index("y")
    high = lax.rem(position, 2) == 1
    first = jnp.where(high, 256, 0) + 8 * lax.div(position, 2)
    step = lax.broadcasted_iota(jnp.int32, (16, COLS), 0)
    wanted = step + jnp.where(step < 8, first, first + 120)
    pick = jnp.where(lax.broadcasted_iota(jnp.int32, (16, COLS), 1) == wanted, 1.0, 0.0)
    slab = slab_ref[...]
    rows = dot(dot(pick, slab, 1, 1), slab, 1, 0)
    for core, row in enumerate((rows[:8], rows[8:])):
        turned = jnp.concatenate([row, row], axis=1)
        near = turned[:, 128 * core : 128 * core + 384]
        far = turned[:, 128 * core + 256 : 128 * core + 640]
        tiles = jnp.where(high, far, near)
        for layer in range(copies_ref.shape[0] // 2):
            copies_ref[2 * layer + core] = tiles


def sum_kernel(parts_ref, copies_ref):
    total = jnp.sum(parts_ref[...], axis=0)
    copies_ref[...] = jnp.broadcast_to(total[None], copies_ref.shape)


def inverse_factor(gram):
    lane = lax.broadcasted_iota(jnp.int32, (8, 128), 1)
    row = lax.broadcasted_iota(jnp.int32, (8, 128), 0)
    blocks = []
    for b in range(8):
        wide = jnp.concatenate([gram[8 * b : 8 * b + 8], jnp.zeros((8, RANK), F32)], axis=1)
        blocks.append(jnp.where(lane == RANK + 8 * b + row, 1.0, wide))

    def spread(part):
        return jnp.broadcast_to(part, (8, 128))

    for p in range(8):
        rows = [spread(blocks[p][i : i + 1]) for i in range(8)]
        entry = {(i, j): spread(rows[i][:, 8 * p + j : 8 * p + j + 1]) for i in range(8) for j in range(i, 8)}
        columns = {
            b: [spread(blocks[b][:, 8 * p + j : 8 * p + j + 1]) for j in range(8)] for b in range(p + 1, 8)
        }
        for i in range(8):
            scale = lax.rsqrt(entry[i, i])
            rows[i] = rows[i] * scale
            for column in columns.values():
                column[i] = column[i] * scale
            factor = {j: entry[i, j] * scale for j in range(i + 1, 8)}
            for k in range(i + 1, 8):
                for j in range(k, 8):
                    entry[k, j] = entry[k, j] - factor[k] * factor[j]
                rows[k] = rows[k] - factor[k] * rows[i]
                for column in columns.values():
                    column[k] = column[k] - factor[k] * column[i]
        for b, column in columns.items():
            for i in range(8):
                blocks[b] = blocks[b] - column[i] * rows[i]
        done = rows[0]
        for i in range(1, 8):
            done = jnp.where(row == i, rows[i], done)
        blocks[p] = done
    return jnp.concatenate([block[:, RANK:] for block in blocks], axis=0)


def final_kernel(tiles_ref, slab_ref, merged_ref, right_ref, left_out, right_out, memory_out, moment):
    for b in range(4):
        for j in range(3):
            block = tiles_ref[b % 2, :, b // 2, :, 128 * j : 128 * j + 128].reshape(128, 128)
            to = (b + j) % 4
            moment[128 * b : 128 * b + 128, 128 * to : 128 * to + 128] = block
            if j == 1:
                moment[128 * to : 128 * to + 128, 128 * b : 128 * b + 128] = block.T
    start = right_ref[...]
    image = dot(start, moment[...], 1, 0)
    right = dot(inverse_factor(dot(start, image, 1, 1)), image, 1, 0)
    image = dot(right, moment[...], 1, 0)
    left_raw = dot(right, slab_ref[...], 1, 1)
    inverse = inverse_factor(dot(right, image, 1, 1))
    left = dot(inverse, left_raw, 1, 0)
    right = dot(inverse, image, 1, 0)
    left_out[...] = math.sqrt(ROWS) * left
    right_out[...] = right
    memory_out[...] = merged_ref[...] - dot(left, right, 0, 0)


def call(kernel, out_shape, flops, moved, scratch=()):
    return pl.pallas_call(
        kernel,
        out_shape=out_shape,
        scratch_shapes=scratch,
        compiler_params=PARAMS,
        cost_estimate=pl.CostEstimate(flops=flops, bytes_accessed=moved, transcendentals=0),
    )


def on_device(tokens_in, out_grad, memory, right_init):
    replicas, layers = lax.axis_size(("x", "y")), lax.axis_size("z")
    rows = lax.axis_size("x")
    pieces = 2 * layers
    tokens = tokens_in.reshape(layers, 2, TOKENS, COLS)
    own = exchange(jnp.broadcast_to(out_grad[None], (layers, TOKENS, COLS)), "z")
    other = lax.ppermute(own, "core", [(0, 1), (1, 0)])
    half = call(functools.partial(gradient_kernel, 0), shape(COLS, COLS), 1 << 29, 1 << 22)
    merged = half(tokens, own, memory[0])
    half = call(functools.partial(gradient_kernel, 1), shape(COLS, COLS), 1 << 29, 1 << 22)
    merged = half(tokens, other, merged)
    parts = exchange(merged.reshape(rows, -1, COLS), "x")
    part = call(partial_kernel, shape(COLS // rows, COLS), 1 << 18, 1 << 20)(parts)
    parts = exchange(part.reshape(replicas // rows, -1, COLS), "y")
    scaled = functools.partial(mean_kernel, replicas)
    copies = call(scaled, shape(replicas // rows, 16, COLS), 1 << 16, 1 << 20)(parts)
    part = exchange(copies, "y").reshape(COLS // rows, COLS)
    slab = exchange(jnp.broadcast_to(part[None], (rows,) + part.shape), "x").reshape(COLS, COLS)
    copies = call(moment_kernel, shape(pieces, 8, 384), 1 << 26, 1 << 20)(slab)
    copies = call(sum_kernel, shape(replicas, 8, 384), 1 << 17, 1 << 20)(exchange(copies, ("z", "core")))
    tiles = lax.all_gather(exchange(copies, ("x", "y")), "core").reshape(2, 16, 2, 8, 384)
    left, right, new_memory = call(
        final_kernel,
        (shape(RANK, COLS), shape(RANK, COLS), shape(COLS, COLS)),
        1 << 28,
        1 << 22,
        [pltpu.VMEM((COLS, COLS), F32)],
    )(tiles, slab, merged, right_init.T)
    return (left.T, right.T, new_memory[None])


def solution(mesh):
    replicas, pieces = mesh.devices.shape
    split = Mesh(mesh.devices.reshape(4, replicas // 4, pieces // 2, 2), ("x", "y", "z", "core"))
    dp, tensor = ("x", "y"), ("z", "core")
    return jax.shard_map(
        on_device,
        mesh=split,
        in_specs=(P(dp, tensor), P(dp + tensor, None), P(dp, tensor, None), P()),
        out_specs=(P(tensor, None), P(), P(dp, tensor, None)),
        check_vma=False,
    )
```

```python
import functools
import math

import jax
import jax.numpy as jnp
from jax import lax
from jax.experimental import pallas as pl
from jax.experimental.pallas import tpu as pltpu
from jax.sharding import Mesh, PartitionSpec as P

ROWS, COLS, RANK, TOKENS = 8192, 512, 64, 152
F32 = jnp.float32
PARAMS = pltpu.CompilerParams(vmem_limit_bytes=32 * 1024 * 1024)


def dot(a, b, ca, cb):
    return lax.dot_general(
        a, b, (((ca,), (cb,)), ((), ())), precision=lax.Precision.HIGHEST, preferred_element_type=F32
    )


def dot3(a, b, ca, cb):
    def halves(v):
        high = v.astype(jnp.bfloat16)
        return high, (v - high.astype(F32)).astype(jnp.bfloat16)

    def one(x, y):
        return lax.dot_general(x, y, (((ca,), (cb,)), ((), ())), preferred_element_type=F32)

    (ah, al), (bh, bl) = halves(a), halves(b)
    return one(ah, bh) + (one(ah, bl) + one(al, bh))


def shape(*dims):
    return jax.ShapeDtypeStruct(dims, F32)


def exchange(pieces, axis):
    return lax.all_to_all(pieces, axis, 0, 0, tiled=False)


def gradient_kernel(flip, tokens_ref, grads_ref, start_ref, out_ref):
    core = lax.axis_index("core")
    side = 1 - core if flip else core
    total = start_ref[...]
    for layer in range(tokens_ref.shape[0]):
        total += lax.dot_general(
            tokens_ref[layer, side], grads_ref[layer], (((0,), (0,)), ((), ())), preferred_element_type=F32
        )
    out_ref[...] = total


def partial_kernel(parts_ref, part_ref):
    part_ref[...] = jnp.sum(parts_ref[...], axis=0)


def mean_kernel(count, parts_ref, copies_ref):
    mean = jnp.sum(parts_ref[...], axis=0) * (1.0 / count)
    copies_ref[...] = jnp.broadcast_to(mean[None], copies_ref.shape)


def moment_kernel(slab_ref, copies_ref):
    position = lax.axis_index("x") * lax.axis_size("y") + lax.axis_index("y")
    high = lax.rem(position, 2) == 1
    back = lax.rem(128 - 8 * lax.div(position, 2), 128)
    slab = slab_ref[...]
    even = pltpu.roll(jnp.where(high, slab[:, 256:384], slab[:, :128]), back, 1)
    odd = pltpu.roll(jnp.where(high, slab[:, 384:], slab[:, 128:256]), lax.rem(back + 8, 128), 1)
    lane = lax.broadcasted_iota(jnp.int32, (COLS, 128), 1)
    rows = dot(jnp.where(lane < 8, even, odd).T[:16], slab, 1, 0)
    for core, row in enumerate((rows[:8], rows[8:])):
        turned = jnp.concatenate([row, row], axis=1)
        near = turned[:, 128 * core : 128 * core + 384]
        far = turned[:, 128 * core + 256 : 128 * core + 640]
        tiles = jnp.where(high, far, near)
        for layer in range(copies_ref.shape[0] // 2):
            copies_ref[2 * layer + core] = tiles


def sum_kernel(parts_ref, copies_ref):
    total = jnp.sum(parts_ref[...], axis=0)
    copies_ref[...] = jnp.broadcast_to(total[None], copies_ref.shape)


def inverse_factor(gram):
    lane = lax.broadcasted_iota(jnp.int32, (8, 128), 1)
    row = lax.broadcasted_iota(jnp.int32, (8, 128), 0)
    blocks = []
    for b in range(8):
        wide = jnp.concatenate([gram[8 * b : 8 * b + 8], jnp.zeros((8, RANK), F32)], axis=1)
        blocks.append(jnp.where(lane == RANK + 8 * b + row, 1.0, wide))

    def spread(part):
        return jnp.broadcast_to(part, (8, 128))

    for p in range(8):
        rows = [spread(blocks[p][i : i + 1]) for i in range(8)]
        entry = {(i, j): spread(rows[i][:, 8 * p + j : 8 * p + j + 1]) for i in range(8) for j in range(i, 8)}
        columns = {
            b: [spread(blocks[b][:, 8 * p + j : 8 * p + j + 1]) for j in range(8)] for b in range(p + 1, 8)
        }
        for i in range(8):
            scale = lax.rsqrt(entry[i, i])
            rows[i] = rows[i] * scale
            for column in columns.values():
                column[i] = column[i] * scale
            factor = {j: entry[i, j] * scale for j in range(i + 1, 8)}
            for k in range(i + 1, 8):
                for j in range(k, 8):
                    entry[k, j] = entry[k, j] - factor[k] * factor[j]
                rows[k] = rows[k] - factor[k] * rows[i]
                for column in columns.values():
                    column[k] = column[k] - factor[k] * column[i]
        for b, column in columns.items():
            for i in range(8):
                blocks[b] = blocks[b] - column[i] * rows[i]
        done = rows[0]
        for i in range(1, 8):
            done = jnp.where(row == i, rows[i], done)
        blocks[p] = done
    return jnp.concatenate([block[:, RANK:] for block in blocks], axis=0)


def final_kernel(tiles_ref, slab_ref, merged_ref, right_ref, left_out, right_out, memory_out, moment):
    for b in range(4):
        for j in range(3):
            block = tiles_ref[b % 2, :, b // 2, :, 128 * j : 128 * j + 128].reshape(128, 128)
            to = (b + j) % 4
            moment[128 * b : 128 * b + 128, 128 * to : 128 * to + 128] = block
            if j == 1:
                moment[128 * to : 128 * to + 128, 128 * b : 128 * b + 128] = block.T
    start = right_ref[...]
    image = dot(start, moment[...], 1, 0)
    right = dot(inverse_factor(dot(start, image, 1, 1)), image, 1, 0)
    image = dot(right, moment[...], 1, 0)
    left_raw = dot3(right, slab_ref[...], 1, 1)
    inverse = inverse_factor(dot(right, image, 1, 1))
    left = dot(inverse, left_raw, 1, 0)
    right = dot(inverse, image, 1, 0)
    left_out[...] = math.sqrt(ROWS) * left
    right_out[...] = right
    memory_out[...] = merged_ref[...] - dot3(left, right, 0, 0)


def call(kernel, out_shape, flops, moved, scratch=()):
    return pl.pallas_call(
        kernel,
        out_shape=out_shape,
        scratch_shapes=scratch,
        compiler_params=PARAMS,
        cost_estimate=pl.CostEstimate(flops=flops, bytes_accessed=moved, transcendentals=0),
    )


def on_device(tokens_in, out_grad, memory, right_init):
    replicas, layers = lax.axis_size(("x", "y")), lax.axis_size("z")
    rows = lax.axis_size("x")
    pieces = 2 * layers
    tokens = tokens_in.reshape(layers, 2, TOKENS, COLS)
    own = exchange(jnp.broadcast_to(out_grad[None], (layers, TOKENS, COLS)), "z")
    other = lax.ppermute(own, "core", [(0, 1), (1, 0)])
    half = call(functools.partial(gradient_kernel, 0), shape(COLS, COLS), 1 << 29, 1 << 22)
    merged = half(tokens, own, memory[0])
    half = call(functools.partial(gradient_kernel, 1), shape(COLS, COLS), 1 << 29, 1 << 22)
    merged = half(tokens, other, merged)
    parts = exchange(merged.reshape(rows, -1, COLS), "x")
    part = call(partial_kernel, shape(COLS // rows, COLS), 1 << 18, 1 << 20)(parts)
    parts = exchange(part.reshape(replicas // rows, -1, COLS), "y")
    scaled = functools.partial(mean_kernel, replicas)
    copies = call(scaled, shape(replicas // rows, 16, COLS), 1 << 16, 1 << 20)(parts)
    part = exchange(copies, "y").reshape(COLS // rows, COLS)
    slab = exchange(jnp.broadcast_to(part[None], (rows,) + part.shape), "x").reshape(COLS, COLS)
    copies = call(moment_kernel, shape(pieces, 8, 384), 1 << 26, 1 << 20)(slab)
    copies = call(sum_kernel, shape(replicas, 8, 384), 1 << 17, 1 << 20)(exchange(copies, ("z", "core")))
    tiles = lax.all_gather(exchange(copies, ("x", "y")), "core").reshape(2, 16, 2, 8, 384)
    left, right, new_memory = call(
        final_kernel,
        (shape(RANK, COLS), shape(RANK, COLS), shape(COLS, COLS)),
        1 << 28,
        1 << 22,
        [pltpu.VMEM((COLS, COLS), F32)],
    )(tiles, slab, merged, right_init.T)
    return (left.T, right.T, new_memory[None])


def solution(mesh):
    replicas, pieces = mesh.devices.shape
    split = Mesh(mesh.devices.reshape(4, replicas // 4, pieces // 2, 2), ("x", "y", "z", "core"))
    dp, tensor = ("x", "y"), ("z", "core")
    return jax.shard_map(
        on_device,
        mesh=split,
        in_specs=(P(dp, tensor), P(dp + tensor, None), P(dp, tensor, None), P()),
        out_specs=(P(tensor, None), P(), P(dp, tensor, None)),
        check_vma=False,
    )
```

```python
import functools
import math

import jax
import jax.numpy as jnp
from jax import lax
from jax.experimental import pallas as pl
from jax.experimental.pallas import tpu as pltpu
from jax.sharding import Mesh, PartitionSpec as P

ROWS, COLS, RANK, TOKENS = 8192, 512, 64, 152
F32 = jnp.float32
PARAMS = pltpu.CompilerParams(vmem_limit_bytes=32 * 1024 * 1024)


def dot(a, b, ca, cb):
    return lax.dot_general(
        a, b, (((ca,), (cb,)), ((), ())), precision=lax.Precision.HIGHEST, preferred_element_type=F32
    )


def dot3(a, b, ca, cb):
    def halves(v):
        high = v.astype(jnp.bfloat16)
        return high, (v - high.astype(F32)).astype(jnp.bfloat16)

    def one(x, y):
        return lax.dot_general(x, y, (((ca,), (cb,)), ((), ())), preferred_element_type=F32)

    (ah, al), (bh, bl) = halves(a), halves(b)
    return one(ah, bh) + (one(ah, bl) + one(al, bh))


def shape(*dims):
    return jax.ShapeDtypeStruct(dims, F32)


def exchange(pieces, axis):
    return lax.all_to_all(pieces, axis, 0, 0, tiled=False)


def gradient_kernel(flip, tokens_ref, grads_ref, start_ref, out_ref):
    core = lax.axis_index("core")
    side = 1 - core if flip else core
    total = start_ref[...]
    for layer in range(tokens_ref.shape[0]):
        total += lax.dot_general(
            tokens_ref[layer, side], grads_ref[layer], (((0,), (0,)), ((), ())), preferred_element_type=F32
        )
    out_ref[...] = total


def partial_kernel(parts_ref, part_ref):
    part_ref[...] = jnp.sum(parts_ref[...], axis=0)


def mean_kernel(count, parts_ref, copies_ref):
    mean = jnp.sum(parts_ref[...], axis=0) * (1.0 / count)
    copies_ref[...] = jnp.broadcast_to(mean[None], copies_ref.shape)


def moment_kernel(slab_ref, copies_ref):
    position = lax.axis_index("x") * lax.axis_size("y") + lax.axis_index("y")
    high = lax.rem(position, 2) == 1
    back = lax.rem(128 - 8 * lax.div(position, 2), 128)
    slab = slab_ref[...]
    even = pltpu.roll(jnp.where(high, slab[:, 256:384], slab[:, :128]), back, 1)
    odd = pltpu.roll(jnp.where(high, slab[:, 384:], slab[:, 128:256]), lax.rem(back + 8, 128), 1)
    lane = lax.broadcasted_iota(jnp.int32, (COLS, 128), 1)
    rows = dot(jnp.where(lane < 8, even, odd).T[:16], slab, 1, 0)
    for core, row in enumerate((rows[:8], rows[8:])):
        turned = jnp.concatenate([row, row], axis=1)
        near = turned[:, 128 * core : 128 * core + 384]
        far = turned[:, 128 * core + 256 : 128 * core + 640]
        tiles = jnp.where(high, far, near)
        for layer in range(copies_ref.shape[0] // 2):
            copies_ref[2 * layer + core] = tiles


def sum_kernel(parts_ref, copies_ref):
    total = jnp.sum(parts_ref[...], axis=0)
    copies_ref[...] = jnp.broadcast_to(total[None], copies_ref.shape)


def inverse_factor(gram):
    lane = lax.broadcasted_iota(jnp.int32, (8, 128), 1)
    row = lax.broadcasted_iota(jnp.int32, (8, 128), 0)
    blocks = []
    for b in range(8):
        wide = jnp.concatenate([gram[8 * b : 8 * b + 8], jnp.zeros((8, RANK), F32)], axis=1)
        blocks.append(jnp.where(lane == RANK + 8 * b + row, 1.0, wide))

    def spread(part):
        return jnp.broadcast_to(part, (8, 128))

    for p in range(8):
        rows = [spread(blocks[p][i : i + 1]) for i in range(8)]
        entry = {(i, j): spread(rows[i][:, 8 * p + j : 8 * p + j + 1]) for i in range(8) for j in range(i, 8)}
        columns = {
            b: [spread(blocks[b][:, 8 * p + j : 8 * p + j + 1]) for j in range(8)] for b in range(p + 1, 8)
        }
        for i in range(8):
            scale = lax.rsqrt(entry[i, i])
            rows[i] = rows[i] * scale
            for column in columns.values():
                column[i] = column[i] * scale
            factor = {j: entry[i, j] * scale for j in range(i + 1, 8)}
            for k in range(i + 1, 8):
                for j in range(k, 8):
                    entry[k, j] = entry[k, j] - factor[k] * factor[j]
                rows[k] = rows[k] - factor[k] * rows[i]
                for column in columns.values():
                    column[k] = column[k] - factor[k] * column[i]
        for b, column in columns.items():
            for i in range(8):
                blocks[b] = blocks[b] - column[i] * rows[i]
        done = rows[0]
        for i in range(1, 8):
            done = jnp.where(row == i, rows[i], done)
        blocks[p] = done
    return jnp.concatenate([block[:, RANK:] for block in blocks], axis=0)


def final_kernel(tiles_ref, slab_ref, merged_ref, right_ref, left_out, right_out, memory_out, moment):
    for b in range(4):
        for j in range(3):
            block = tiles_ref[b % 2, :, b // 2, :, 128 * j : 128 * j + 128].reshape(128, 128)
            to = (b + j) % 4
            moment[128 * b : 128 * b + 128, 128 * to : 128 * to + 128] = block
            if j == 1:
                moment[128 * to : 128 * to + 128, 128 * b : 128 * b + 128] = block.T
    start = right_ref[...]
    image = dot(start, moment[...], 1, 0)
    right = dot(inverse_factor(dot(start, image, 1, 1)), image, 1, 0)
    image = dot(right, moment[...], 1, 0)
    left_raw = dot3(right, slab_ref[...], 1, 1)
    inverse = inverse_factor(dot(right, image, 1, 1))
    left = dot(inverse, left_raw, 1, 0)
    right = dot(inverse, image, 1, 0)
    left_out[...] = math.sqrt(ROWS) * left
    right_out[...] = right
    memory_out[...] = merged_ref[...] - dot3(left, right, 0, 0)


def call(kernel, out_shape, flops, moved, scratch=()):
    return pl.pallas_call(
        kernel,
        out_shape=out_shape,
        scratch_shapes=scratch,
        compiler_params=PARAMS,
        cost_estimate=pl.CostEstimate(flops=flops, bytes_accessed=moved, transcendentals=0),
    )


def on_device(tokens_in, out_grad, memory, right_init):
    replicas, layers = lax.axis_size(("x", "y")), lax.axis_size(("zh", "zl"))
    rows = lax.axis_size("x")
    pieces = 2 * layers
    tokens = tokens_in.reshape(layers, 2, TOKENS, COLS)
    pair = exchange(jnp.broadcast_to(out_grad[None], (2, TOKENS, COLS)), "zl")
    own = exchange(jnp.broadcast_to(pair[None], (layers // 2,) + pair.shape), "zh").reshape(layers, TOKENS, COLS)
    other = lax.ppermute(own, "core", [(0, 1), (1, 0)])
    half = call(functools.partial(gradient_kernel, 0), shape(COLS, COLS), 1 << 29, 1 << 22)
    merged = half(tokens, own, memory[0])
    half = call(functools.partial(gradient_kernel, 1), shape(COLS, COLS), 1 << 29, 1 << 22)
    merged = half(tokens, other, merged)
    parts = exchange(merged.reshape(rows, -1, COLS), "x")
    part = call(partial_kernel, shape(COLS // rows, COLS), 1 << 18, 1 << 20)(parts)
    parts = exchange(part.reshape(replicas // rows, -1, COLS), "y")
    scaled = functools.partial(mean_kernel, replicas)
    copies = call(scaled, shape(replicas // rows, 16, COLS), 1 << 16, 1 << 20)(parts)
    part = exchange(copies, "y").reshape(COLS // rows, COLS)
    slab = exchange(jnp.broadcast_to(part[None], (rows,) + part.shape), "x").reshape(COLS, COLS)
    copies = call(moment_kernel, shape(pieces, 8, 384), 1 << 26, 1 << 20)(slab)
    copies = call(sum_kernel, shape(replicas, 8, 384), 1 << 17, 1 << 20)(exchange(copies, ("zh", "zl", "core")))
    tiles = lax.all_gather(exchange(copies, ("x", "y")), "core").reshape(2, 16, 2, 8, 384)
    left, right, new_memory = call(
        final_kernel,
        (shape(RANK, COLS), shape(RANK, COLS), shape(COLS, COLS)),
        1 << 28,
        1 << 22,
        [pltpu.VMEM((COLS, COLS), F32)],
    )(tiles, slab, merged, right_init.T)
    return (left.T, right.T, new_memory[None])


def solution(mesh):
    replicas, pieces = mesh.devices.shape
    split = Mesh(mesh.devices.reshape(4, replicas // 4, pieces // 4, 2, 2), ("x", "y", "zh", "zl", "core"))
    dp, tensor = ("x", "y"), ("zh", "zl", "core")
    return jax.shard_map(
        on_device,
        mesh=split,
        in_specs=(P(dp, tensor), P(dp + tensor, None), P(dp, tensor, None), P()),
        out_specs=(P(tensor, None), P(), P(dp, tensor, None)),
        check_vma=False,
    )
```

```python
import functools
import math

import jax
import jax.numpy as jnp
from jax import lax
from jax.experimental import pallas as pl
from jax.experimental.pallas import tpu as pltpu
from jax.sharding import Mesh, PartitionSpec as P

ROWS, COLS, RANK, TOKENS = 8192, 512, 64, 152
F32 = jnp.float32
PARAMS = pltpu.CompilerParams(vmem_limit_bytes=32 * 1024 * 1024)


def dot(a, b, ca, cb):
    return lax.dot_general(
        a, b, (((ca,), (cb,)), ((), ())), precision=lax.Precision.HIGHEST, preferred_element_type=F32
    )


def dot3(a, b, ca, cb):
    def halves(v):
        high = v.astype(jnp.bfloat16)
        return high, (v - high.astype(F32)).astype(jnp.bfloat16)

    def one(x, y):
        return lax.dot_general(x, y, (((ca,), (cb,)), ((), ())), preferred_element_type=F32)

    (ah, al), (bh, bl) = halves(a), halves(b)
    return one(ah, bh) + (one(ah, bl) + one(al, bh))


def shape(*dims):
    return jax.ShapeDtypeStruct(dims, F32)


def exchange(pieces, axis):
    return lax.all_to_all(pieces, axis, 0, 0, tiled=False)


def gradient_kernel(flip, tokens_ref, grads_ref, start_ref, out_ref):
    core = lax.axis_index("core")
    side = 1 - core if flip else core
    total = start_ref[...]
    for layer in range(tokens_ref.shape[0]):
        total += lax.dot_general(
            tokens_ref[layer, side], grads_ref[layer], (((0,), (0,)), ((), ())), preferred_element_type=F32
        )
    out_ref[...] = total


def partial_kernel(parts_ref, part_ref):
    part_ref[...] = jnp.sum(parts_ref[...], axis=0)


def mean_kernel(count, parts_ref, copies_ref):
    mean = jnp.sum(parts_ref[...], axis=0) * (1.0 / count)
    copies_ref[...] = jnp.broadcast_to(mean[None], copies_ref.shape)


def moment_kernel(slab_ref, copies_ref):
    position = lax.axis_index("x") * lax.axis_size("y") + lax.axis_index("y")
    high = lax.rem(position, 2) == 1
    back = lax.rem(128 - 8 * lax.div(position, 2), 128)
    slab = slab_ref[...]
    even = pltpu.roll(jnp.where(high, slab[:, 256:384], slab[:, :128]), back, 1)
    odd = pltpu.roll(jnp.where(high, slab[:, 384:], slab[:, 128:256]), lax.rem(back + 8, 128), 1)
    lane = lax.broadcasted_iota(jnp.int32, (COLS, 128), 1)
    rows = dot(jnp.where(lane < 8, even, odd).T[:16], slab, 1, 0)
    for core, row in enumerate((rows[:8], rows[8:])):
        turned = jnp.concatenate([row, row], axis=1)
        near = turned[:, 128 * core : 128 * core + 384]
        far = turned[:, 128 * core + 256 : 128 * core + 640]
        tiles = jnp.where(high, far, near)
        for layer in range(copies_ref.shape[0] // 2):
            copies_ref[2 * layer + core] = tiles


def sum_kernel(parts_ref, copies_ref):
    total = jnp.sum(parts_ref[...], axis=0)
    copies_ref[...] = jnp.broadcast_to(total[None], copies_ref.shape)


def inverse_factor(gram):
    lane = lax.broadcasted_iota(jnp.int32, (8, 128), 1)
    row = lax.broadcasted_iota(jnp.int32, (8, 128), 0)
    blocks = []
    for b in range(8):
        wide = jnp.concatenate([gram[8 * b : 8 * b + 8], jnp.zeros((8, RANK), F32)], axis=1)
        blocks.append(jnp.where(lane == RANK + 8 * b + row, 1.0, wide))

    def spread(part):
        return jnp.broadcast_to(part, (8, 128))

    for p in range(8):
        rows = [spread(blocks[p][i : i + 1]) for i in range(8)]
        entry = {(i, j): spread(rows[i][:, 8 * p + j : 8 * p + j + 1]) for i in range(8) for j in range(i, 8)}
        columns = {
            b: [spread(blocks[b][:, 8 * p + j : 8 * p + j + 1]) for j in range(8)] for b in range(p + 1, 8)
        }
        for i in range(8):
            scale = lax.rsqrt(entry[i, i])
            rows[i] = rows[i] * scale
            for column in columns.values():
                column[i] = column[i] * scale
            factor = {j: entry[i, j] * scale for j in range(i + 1, 8)}
            for k in range(i + 1, 8):
                for j in range(k, 8):
                    entry[k, j] = entry[k, j] - factor[k] * factor[j]
                rows[k] = rows[k] - factor[k] * rows[i]
                for column in columns.values():
                    column[k] = column[k] - factor[k] * column[i]
        for b, column in columns.items():
            for i in range(8):
                blocks[b] = blocks[b] - column[i] * rows[i]
        done = rows[0]
        for i in range(1, 8):
            done = jnp.where(row == i, rows[i], done)
        blocks[p] = done
    return jnp.concatenate([block[:, RANK:] for block in blocks], axis=0)


def final_kernel(tiles_ref, slab_ref, merged_ref, right_ref, left_out, right_out, memory_out, moment):
    for b in range(4):
        for j in range(3):
            block = tiles_ref[b % 2, :, b // 2, :, 128 * j : 128 * j + 128].reshape(128, 128)
            to = (b + j) % 4
            moment[128 * b : 128 * b + 128, 128 * to : 128 * to + 128] = block
            if j == 1:
                moment[128 * to : 128 * to + 128, 128 * b : 128 * b + 128] = block.T
    start = right_ref[...]
    image = dot(start, moment[...], 1, 0)
    right = dot(inverse_factor(dot(start, image, 1, 1)), image, 1, 0)
    image = dot(right, moment[...], 1, 0)
    left_raw = dot3(right, slab_ref[...], 1, 1)
    inverse = inverse_factor(dot(right, image, 1, 1))
    left = dot(inverse, left_raw, 1, 0)
    right = dot(inverse, image, 1, 0)
    left_out[...] = math.sqrt(ROWS) * left
    right_out[...] = right
    memory_out[...] = merged_ref[...] - dot3(left, right, 0, 0)


def call(kernel, out_shape, flops, moved, scratch=()):
    return pl.pallas_call(
        kernel,
        out_shape=out_shape,
        scratch_shapes=scratch,
        compiler_params=PARAMS,
        cost_estimate=pl.CostEstimate(flops=flops, bytes_accessed=moved, transcendentals=0),
    )


def on_device(tokens_in, out_grad, memory, right_init):
    replicas, layers = lax.axis_size(("x", "y")), lax.axis_size("z")
    rows = lax.axis_size("x")
    pieces = 2 * layers
    tokens = tokens_in.reshape(layers, 2, TOKENS, COLS)
    own = exchange(jnp.broadcast_to(out_grad[None], (layers, TOKENS, COLS)), "z")
    other = lax.ppermute(own, "core", [(0, 1), (1, 0)])
    half = call(functools.partial(gradient_kernel, 0), shape(COLS, COLS), 1 << 29, 1 << 22)
    merged = half(tokens, own, memory[0])
    half = call(functools.partial(gradient_kernel, 1), shape(COLS, COLS), 1 << 29, 1 << 22)
    merged = half(tokens, other, merged)
    parts = exchange(merged.reshape(rows, -1, COLS), "x")
    part = call(partial_kernel, shape(COLS // rows, COLS), 1 << 18, 1 << 20)(parts)
    parts = exchange(part.reshape(replicas // rows, -1, COLS), "y")
    scaled = functools.partial(mean_kernel, replicas)
    copies = call(scaled, shape(replicas // rows, 16, COLS), 1 << 16, 1 << 20)(parts)
    part = exchange(copies, "y").reshape(COLS // rows, COLS)
    slab = exchange(jnp.broadcast_to(part[None], (rows,) + part.shape), "x").reshape(COLS, COLS)
    copies = call(moment_kernel, shape(pieces, 8, 384), 1 << 26, 1 << 20)(slab)
    columns = replicas // rows
    copies = call(sum_kernel, shape(columns, 8, 384), 1 << 17, 1 << 20)(exchange(copies, ("z", "core")))
    part = exchange(copies, "y")
    tiles = exchange(jnp.broadcast_to(part[None], (rows,) + part.shape), "x")
    tiles = lax.all_gather(tiles.reshape(replicas, 8, 384), "core").reshape(2, 16, 2, 8, 384)
    left, right, new_memory = call(
        final_kernel,
        (shape(RANK, COLS), shape(RANK, COLS), shape(COLS, COLS)),
        1 << 28,
        1 << 22,
        [pltpu.VMEM((COLS, COLS), F32)],
    )(tiles, slab, merged, right_init.T)
    return (left.T, right.T, new_memory[None])


def solution(mesh):
    replicas, pieces = mesh.devices.shape
    split = Mesh(mesh.devices.reshape(4, replicas // 4, pieces // 2, 2), ("x", "y", "z", "core"))
    dp, tensor = ("x", "y"), ("z", "core")
    return jax.shard_map(
        on_device,
        mesh=split,
        in_specs=(P(dp, tensor), P(dp + tensor, None), P(dp, tensor, None), P()),
        out_specs=(P(tensor, None), P(), P(dp, tensor, None)),
        check_vma=False,
    )
```
